128 devices in a mesh: tm: 4 (over y_hi, core), chan: 32 (over y_lo, x, z).
Axes of the slice: x: 4, y: 4 (y_hi: 2, y_lo: 2; y = y_hi * 2 + y_lo), z: 4, core: 2. Of those that a mesh axis runs over, the one named last changes fastest.
Arguments:
- samples: bfloat16 [2048, 262144], P('chan', 'tm'), may hold values from -6 to 6
- tap_weights: float32 [16, 2048], replicated, may hold values from -1.5 to 1.5
Outputs:
- visibilities: bfloat16 [128, 2, 2048, 2048], P('chan', None, 'tm')
The draws below stay inside these ranges and needn't reach their ends.
All inputs are finite; a program needn't handle non-finite values.
Results may differ from the reference program's by a relative error of at most 0.012.
Values may be sent and summed in bfloat16 or wider, within the bound.
No kernel may reach another device: no remote copies, remote signals or barrier semaphores. Data moves between devices by JAX's collectives and lax.ppermute only.
A program may use at most 320 MiB of HBM per device.

```python
import math
import jax
import jax.numpy as jnp
from jax import lax

S = 2048
NFFT = 2048
TAPS = 16
CH0 = 256
FR_DEV = 32
CH_DEV = 4
SAMPLES = 262144
N_TM = 4
N_CHAN = 32


def block_levels(key, shape, shards, least, largest):
    def one(position, parts):
        heights = jax.random.uniform(jax.random.fold_in(jax.random.fold_in(key, 6), position), (parts,), jnp.float32, least / len(shards), largest / len(shards))
        return jnp.repeat(jnp.exp(heights), shape[position] // parts).reshape((-1,) + (1,) * (len(shape) - position - 1))

    factor_of = one(*shards[0])
    for cut in shards[1:]:
        factor_of = factor_of * one(*cut)
    return factor_of


def centred(stream_key, shape, spread, most, pieces=(), kind=jnp.bfloat16):
    loudness = block_levels(stream_key, shape, pieces, -0.22, 0.18) if pieces else 1.0
    entries = jax.random.normal(stream_key, shape, jnp.float32) * spread * loudness
    return jnp.minimum(jnp.maximum(entries, -most), most).astype(kind)


def setup_inputs(seed: int = 0) -> dict:
    seeds = jax.random.split(jax.random.key(seed), 3)
    return {
        "samples": centred(seeds[0], (S, SAMPLES), 1.0, 6.0, ((0, 32), (1, 4))),
        "tap_weights": centred(seeds[1], (TAPS, NFFT), 0.25, 1.5, (), jnp.float32),
    }


def make_table():
    band_count = CH_DEV * N_CHAN
    sample = jnp.arange(NFFT, dtype=jnp.int32)
    channel = CH0 + jnp.arange(band_count, dtype=jnp.int32)
    phase_index = sample[:, None] * channel[None, :] % NFFT
    angle_rad = phase_index.astype(jnp.float32) * (2.0 * math.pi / NFFT)
    norm_scale = 1.0 / math.sqrt(NFFT)
    return jnp.concatenate([jnp.cos(angle_rad) * norm_scale, -jnp.sin(angle_rad) * norm_scale], axis=1)

def reference(samples, tap_weights):
    band_count = CH_DEV * N_CHAN
    frames_all = FR_DEV * N_TM
    group_size = S // N_CHAN
    dft_table = make_table()
    blocks = samples.reshape(N_CHAN, group_size, frames_all, NFFT)

    def spectra(signal_rows):
        zero_head = jnp.zeros((group_size, TAPS - 1, NFFT), signal_rows.dtype)
        extended = jnp.concatenate([zero_head, signal_rows], axis=1)
        summed = jnp.zeros((group_size, frames_all, NFFT), jnp.float32)
        for tap_index in range(TAPS):
            summed = summed + extended[:, tap_index:tap_index + frames_all].astype(jnp.float32) * tap_weights[tap_index]
        filtered = summed.reshape(group_size * frames_all, NFFT)
        return jnp.dot(filtered, dft_table, precision=lax.Precision.HIGHEST, preferred_element_type=jnp.float32).astype(jnp.bfloat16)
    voltages = lax.map(spectra, blocks).reshape(S, frames_all, 2 * band_count)
    real_all = jnp.transpose(voltages[:, :, :band_count], (2, 0, 1))
    imag_all = jnp.transpose(voltages[:, :, band_count:], (2, 0, 1))

    def correlate(parts_pair):
        real_part, imag_part = parts_pair
        left_rows = jnp.concatenate([real_part, imag_part], axis=1)
        turned = jnp.concatenate([imag_part, -real_part], axis=1)
        power_sum = jnp.dot(left_rows, left_rows.T, preferred_element_type=jnp.float32)
        cross_sum = jnp.dot(turned, left_rows.T, preferred_element_type=jnp.float32)
        return (jnp.stack([power_sum, cross_sum]) * (1.0 / frames_all)).astype(jnp.bfloat16)
    return lax.map(correlate, (real_all, imag_all))
```

```python
import functools
import math

import jax
import jax.numpy as jnp
import numpy as np
from jax import lax
from jax.experimental import pallas as pl
from jax.experimental.pallas import tpu as pltpu
from jax.sharding import Mesh
from jax.sharding import PartitionSpec as P

NFFT = 2048
TAPS = 16
CH0 = 256
CH_DEV = 4
GROUPS = 32
COLS = GROUPS * CH_DEV * 2
SIG = 64
FRAMES = 32
HALF = 16
NT = 512
MIB = 2**20
PEERS = ("yh", "yl", "x", "z")


def dft_columns():
    col = np.arange(COLS)
    channel = CH0 + col // 2
    m = (np.arange(NFFT)[:, None] * channel[None, :]) % NFFT
    angle = m * (2.0 * math.pi / NFFT)
    table = np.where((col % 2 == 0)[None, :], np.cos(angle), -np.sin(angle)) / math.sqrt(NFFT)
    return jnp.asarray(table.astype(np.float32)).astype(jnp.bfloat16)


def pair_sum(terms):
    terms = list(terms)
    while len(terms) > 1:
        terms = [
            terms[i] + terms[i + 1] if i + 1 < len(terms) else terms[i]
            for i in range(0, len(terms), 2)
        ]
    return terms[0]


def accumulate(first_in, count_in, first_out, x_ref, w_ref, d_ref, filt_ref, acc_ref):
    weights = [
        jnp.broadcast_to(w_ref[p : p + 1, :], (8, NT)).astype(jnp.bfloat16) for p in range(TAPS)
    ]

    def group(s, carry):
        held = {}
        rows = []
        for g in range(first_out, first_out + HALF):
            frames = [f for f in range(g - TAPS + 1, g + 1) if first_in <= f < first_in + count_in]
            for f in frames:
                if f not in held:
                    held[f] = x_ref[s, f - first_in]
            if frames:
                rows.append(pair_sum(held[f] * weights[f - g + TAPS - 1] for f in frames))
            else:
                rows.append(jnp.zeros((8, NT), jnp.bfloat16))
        for k in range(HALF):
            filt_ref[k, s] = rows[k]
        return carry

    lax.fori_loop(0, SIG // 8, group, 0, unroll=8)

    def frames_part(k, carry):
        part = jnp.dot(
            filt_ref[pl.ds(k * 4, 4)].reshape(4 * SIG, NT),
            d_ref[...],
            preferred_element_type=jnp.float32,
        )
        acc_ref[pl.ds(k * 4, 4)] += part.reshape(4, SIG, COLS)
        return carry

    lax.fori_loop(0, HALF // 4, frames_part, 0, unroll=True)


def tail_kernel(first_in, count_in, x_ref, w_ref, d_ref, o_ref, filt_ref, acc_ref):
    @pl.when(pl.program_id(0) == 0)
    def _():
        acc_ref[...] = jnp.zeros_like(acc_ref)

    accumulate(first_in, count_in, FRAMES, x_ref, w_ref, d_ref, filt_ref, acc_ref)

    @pl.when(pl.program_id(0) == pl.num_programs(0) - 1)
    def _():
        o_ref[...] = acc_ref[...].astype(o_ref.dtype)


def emit(acc_ref, turn_ref, o_ref):
    for k in range(HALF // 2):
        block = acc_ref[2 * k : 2 * k + 2].reshape(2 * SIG, COLS)
        turn_ref[pl.ds(k, COLS, stride=HALF // 2), :] = block.T
    value = turn_ref[...].astype(o_ref.dtype).reshape(GROUPS, 64, 128)
    o_ref[0, :, 0] = value
    o_ref[1, :, 0] = value


def late_kernel(x_ref, w_ref, d_ref, o_ref, filt_ref, acc_ref, turn_ref):
    @pl.when(pl.program_id(0) == 0)
    def _():
        acc_ref[...] = jnp.zeros_like(acc_ref)

    accumulate(0, FRAMES, HALF, x_ref, w_ref, d_ref, filt_ref, acc_ref)

    @pl.when(pl.program_id(0) == pl.num_programs(0) - 1)
    def _():
        emit(acc_ref, turn_ref, o_ref)


def early_kernel(x_ref, w_ref, d_ref, halo_ref, late_ref, o_ref, filt_ref, acc_ref, turn_ref):
    del late_ref

    @pl.when(pl.program_id(0) == 0)
    def _():
        acc_ref[...] = halo_ref[...].astype(jnp.float32)

    accumulate(0, HALF, 0, x_ref, w_ref, d_ref, filt_ref, acc_ref)

    @pl.when(pl.program_id(0) == pl.num_programs(0) - 1)
    def _():
        emit(acc_ref, turn_ref, o_ref)


def slab_specs(count_in, block):
    return [
        pl.BlockSpec((SIG // 8, count_in, 8, NT), lambda i: (0, block, 0, i)),
        pl.BlockSpec((TAPS, NT), lambda i: (0, i)),
        pl.BlockSpec((NT, COLS), lambda i: (i, 0)),
    ]


def params():
    return pltpu.CompilerParams(vmem_limit_bytes=48 * MIB)


def filt_shape():
    return pltpu.VMEM((HALF, SIG // 8, 8, NT), jnp.bfloat16)


def acc_shape():
    return pltpu.VMEM((HALF, SIG, COLS), jnp.float32)


def turn_shape():
    return pltpu.VMEM((COLS * HALF // 2, 128), jnp.float32)


def spectra_tail(x4, taps, table):
    return pl.pallas_call(
        functools.partial(tail_kernel, HALF, HALF),
        grid=(NFFT // NT,),
        in_specs=slab_specs(HALF, 1),
        out_specs=pl.BlockSpec((HALF, SIG, COLS), lambda i: (0, 0, 0)),
        out_shape=jax.ShapeDtypeStruct((HALF, SIG, COLS), jnp.bfloat16),
        scratch_shapes=[filt_shape(), acc_shape()],
        compiler_params=params(),
        cost_estimate=pl.CostEstimate(flops=600_000_000, bytes_accessed=6 * MIB, transcendentals=0),
        name="spectra_tail",
    )(x4, taps, table)


VOLT_SHAPE = (2, GROUPS, 2, 64, 128)


def spectra_late(x4, taps, table):
    return pl.pallas_call(
        late_kernel,
        grid=(NFFT // NT,),
        in_specs=slab_specs(FRAMES, 0),
        out_specs=pl.BlockSpec((2, GROUPS, 1, 64, 128), lambda i: (0, 0, 1, 0, 0)),
        out_shape=jax.ShapeDtypeStruct(VOLT_SHAPE, jnp.bfloat16),
        scratch_shapes=[filt_shape(), acc_shape(), turn_shape()],
        compiler_params=params(),
        cost_estimate=pl.CostEstimate(flops=2_000_000_000, bytes_accessed=11 * MIB, transcendentals=0),
        name="spectra_late",
    )(x4, taps, table)


def spectra_early(x4, taps, table, halo, late):
    return pl.pallas_call(
        early_kernel,
        grid=(NFFT // NT,),
        in_specs=slab_specs(HALF, 0)
        + [
            pl.BlockSpec((HALF, SIG, COLS), lambda i: (0, 0, 0)),
            pl.BlockSpec(memory_space=pl.ANY),
        ],
        out_specs=pl.BlockSpec((2, GROUPS, 1, 64, 128), lambda i: (0, 0, 0, 0, 0)),
        out_shape=jax.ShapeDtypeStruct(VOLT_SHAPE, jnp.bfloat16),
        scratch_shapes=[filt_shape(), acc_shape(), turn_shape()],
        input_output_aliases={4: 0},
        compiler_params=params(),
        cost_estimate=pl.CostEstimate(flops=600_000_000, bytes_accessed=7 * MIB, transcendentals=0),
        name="spectra_early",
    )(x4, taps, table, halo, late)


def correlate_kernel(scale, tm_ref, own_ref, other_ref, o_ref, all_ref, left_ref):
    pairs = GROUPS // 2

    @pl.when(pl.program_id(1) == 0)
    def _():
        def gather(q, carry):
            at = pl.ds(pl.multiple_of(q * 128, 128), 128)
            for c, ref in enumerate((own_ref, other_ref)):
                for y in range(2):
                    for h in range(2):
                        t0 = ref[y * GROUPS + 2 * q, h, 0]
                        t1 = ref[y * GROUPS + 2 * q + 1, h, 0]
                        even = jnp.concatenate([t0[:, :SIG], t1[:, :SIG]], axis=1)
                        odd = jnp.concatenate([t0[:, SIG:], t1[:, SIG:]], axis=1)
                        k = ((c * 2 + y) * 2 + h) * 16
                        all_ref[k : k + 16, at] = jnp.concatenate([even[:8], odd[:8]], axis=0)
                        all_ref[128 + k : 144 + k, at] = jnp.concatenate(
                            [even[8:], odd[8:]], axis=0
                        )
            return carry

        lax.fori_loop(0, pairs, gather, 0, unroll=16)
        mine = pl.ds(pl.multiple_of(tm_ref[0] * 512, 512), 512)
        rows = all_ref[:, mine].T
        left_ref[:512] = rows
        left_ref[512:, :128] = rows[:, 128:]
        left_ref[512:, 128:] = -rows[:, :128]

    width = o_ref.shape[-1]
    first = pl.program_id(1) * width

    def columns(n, carry):
        from_ = pl.ds(pl.multiple_of(first + n * 256, 256), 256)
        to = pl.ds(pl.multiple_of(n * 256, 256), 256)
        both = jnp.dot(left_ref[...], all_ref[:, from_], preferred_element_type=jnp.float32)
        both = (both * scale).astype(jnp.bfloat16)
        o_ref[0, 0, :, to] = both[:512]
        o_ref[0, 1, :, to] = both[512:]
        return carry

    lax.fori_loop(0, width // 256, columns, 0, unroll=8)


def correlate(tm, own, other, signals, frames_all):
    shape = (2 * GROUPS, 2, CH_DEV, 16, 128)
    block = pl.BlockSpec((2 * GROUPS, 2, 1, 16, 128), lambda j, n, t: (0, 0, j, 0, 0))
    width = signals // 1
    return pl.pallas_call(
        functools.partial(correlate_kernel, 1.0 / frames_all),
        grid_spec=pltpu.PrefetchScalarGridSpec(
            num_scalar_prefetch=1,
            grid=(CH_DEV, signals // width),
            in_specs=[block, block],
            out_specs=pl.BlockSpec((1, 2, 512, width), lambda j, n, t: (j, 0, 0, n)),
            scratch_shapes=[
                pltpu.VMEM((256, signals), jnp.bfloat16),
                pltpu.VMEM((1024, 256), jnp.bfloat16),
            ],
        ),
        out_shape=jax.ShapeDtypeStruct((CH_DEV, 2, 512, signals), jnp.bfloat16),
        compiler_params=params(),
        cost_estimate=pl.CostEstimate(flops=4_300_000_000, bytes_accessed=20 * MIB, transcendentals=0),
        name="correlate",
    )(tm, own.reshape(shape), other.reshape(shape))


def per_device(samples, tap_weights):
    x4 = samples.reshape(SIG // 8, 8, FRAMES, NFFT).transpose(0, 2, 1, 3)
    table = dft_columns()
    tail = spectra_tail(x4, tap_weights, table)
    halo = lax.ppermute(tail, ("yh", "core"), [(0, 1), (1, 2), (2, 3)])
    late = spectra_late(x4, tap_weights, table)
    volts = spectra_early(x4, tap_weights, table, halo, late)
    volts = volts.reshape(2 * GROUPS, 128, 128)
    own = lax.all_to_all(volts, PEERS, split_axis=0, concat_axis=0, tiled=True)
    other = lax.ppermute(own, "core", [(0, 1), (1, 0)])
    tm = (lax.axis_index("yh") * 2 + lax.axis_index("core")).astype(jnp.int32).reshape(1)
    return correlate(tm, own, other, GROUPS * SIG, FRAMES * 4)


def solution(mesh):
    fine = Mesh(
        mesh.devices.reshape(2, 2, 2, 4, 4),
        ("yh", "core", "yl", "x", "z"),
    )
    return jax.shard_map(
        per_device,
        mesh=fine,
        in_specs=(P(("yl", "x", "z"), ("yh", "core")), P()),
        out_specs=P(("yl", "x", "z"), None, ("yh", "core"), None),
        check_vma=False,
    )
```

```python
import functools
import math

import jax
import jax.numpy as jnp
import numpy as np
from jax import lax
from jax.experimental import pallas as pl
from jax.experimental.pallas import tpu as pltpu
from jax.sharding import Mesh
from jax.sharding import PartitionSpec as P

NFFT = 2048
TAPS = 16
CH0 = 256
CH_DEV = 4
GROUPS = 32
COLS = GROUPS * CH_DEV * 2
SIG = 64
FRAMES = 32
HALF = 16
NT = 512
LANES = 256
SEND = 4
MIB = 2**20
TAIL_MIB = 48
PEERS = ("yh", "yl", "x", "z")


def dft_columns():
    col = np.arange(COLS)
    channel = CH0 + col // 2
    m = (np.arange(NFFT)[:, None] * channel[None, :]) % NFFT
    angle = m * (2.0 * math.pi / NFFT)
    table = np.where((col % 2 == 0)[None, :], np.cos(angle), -np.sin(angle)) / math.sqrt(NFFT)
    return jnp.asarray(table.astype(np.float32)).astype(jnp.bfloat16)


def pair_sum(terms):
    terms = list(terms)
    while len(terms) > 1:
        terms = [
            terms[i] + terms[i + 1] if i + 1 < len(terms) else terms[i]
            for i in range(0, len(terms), 2)
        ]
    return terms[0]


def accumulate(first_in, count_in, first_out, count_out, x_ref, w_ref, d_ref, filt_ref, acc_ref):
    for n in range(0, NT, LANES):
        lanes = slice(n, n + LANES)
        weights = [
            jnp.broadcast_to(w_ref[p : p + 1, lanes], (8, LANES)).astype(jnp.bfloat16)
            for p in range(TAPS)
        ]
        for s in range(SIG // 8):
            held = {}
            for g in range(first_out, first_out + count_out):
                frames = [
                    f for f in range(g - TAPS + 1, g + 1) if first_in <= f < first_in + count_in
                ]
                held = {
                    f: held[f] if f in held else x_ref[s, f - first_in, :, lanes] for f in frames
                }
                if frames:
                    row = pair_sum(held[f] * weights[f - g + TAPS - 1] for f in frames)
                else:
                    row = jnp.zeros((8, LANES), jnp.bfloat16)
                filt_ref[g - first_out, s, :, lanes] = row
    for k in range(0, count_out, 4):
        part = jnp.dot(
            filt_ref[k : k + 4].reshape(4 * SIG, NT),
            d_ref[...],
            preferred_element_type=jnp.float32,
        )
        acc_ref[k : k + 4] += part.reshape(4, SIG, COLS)


def tail_kernel(first_in, count_in, x_ref, w_ref, d_ref, o_ref, filt_ref, acc_ref):
    @pl.when(pl.program_id(0) == 0)
    def _():
        acc_ref[...] = jnp.zeros_like(acc_ref)

    accumulate(first_in, count_in, FRAMES, HALF, x_ref, w_ref, d_ref, filt_ref, acc_ref)

    @pl.when(pl.program_id(0) == pl.num_programs(0) - 1)
    def _():
        o_ref[...] = acc_ref[...].astype(o_ref.dtype)


def emit(acc, turn_ref, o_ref):
    for k in range(HALF // 2):
        block = acc(2 * k).reshape(2 * SIG, COLS)
        turn_ref[pl.ds(k, COLS, stride=HALF // 2), :] = block.T
    value = turn_ref[...].astype(o_ref.dtype).reshape(GROUPS, 64, 128)
    o_ref[0, :, 0] = value
    o_ref[1, :, 0] = value


def main_kernel(x_ref, w_ref, d_ref, o_ref, early_ref, filt_ref, acc_ref, turn_ref):
    @pl.when(pl.program_id(0) == 0)
    def _():
        acc_ref[...] = jnp.zeros_like(acc_ref)

    accumulate(0, FRAMES, 0, FRAMES, x_ref, w_ref, d_ref, filt_ref, acc_ref)

    @pl.when(pl.program_id(0) == pl.num_programs(0) - 1)
    def _():
        early_ref[...] = acc_ref[:HALF]
        emit(lambda k: acc_ref[HALF + k : HALF + k + 2], turn_ref, o_ref)


def join_kernel(early_ref, halo_ref, late_ref, o_ref, turn_ref):
    del late_ref
    emit(
        lambda k: early_ref[k : k + 2] + halo_ref[k : k + 2].astype(jnp.float32), turn_ref, o_ref
    )


def slab_specs(count_in, block):
    return [
        pl.BlockSpec((SIG // 8, count_in, 8, NT), lambda i: (0, block, 0, i)),
        pl.BlockSpec((TAPS, NT), lambda i: (0, i)),
        pl.BlockSpec((NT, COLS), lambda i: (i, 0)),
    ]


def params(mib=48):
    return pltpu.CompilerParams(vmem_limit_bytes=mib * MIB)


def filt_shape(frames):
    return pltpu.VMEM((frames, SIG // 8, 8, NT), jnp.bfloat16)


def acc_shape(frames):
    return pltpu.VMEM((frames, SIG, COLS), jnp.float32)


def turn_shape():
    return pltpu.VMEM((COLS * HALF // 2, 128), jnp.float32)


def spectra_tail(x4, taps, table):
    return pl.pallas_call(
        functools.partial(tail_kernel, HALF, HALF),
        grid=(NFFT // NT,),
        in_specs=slab_specs(HALF, 1),
        out_specs=pl.BlockSpec((HALF, SIG, COLS), lambda i: (0, 0, 0)),
        out_shape=jax.ShapeDtypeStruct((HALF, SIG, COLS), jnp.bfloat16),
        scratch_shapes=[filt_shape(HALF), acc_shape(HALF)],
        compiler_params=params(TAIL_MIB),
        cost_estimate=pl.CostEstimate(flops=600_000_000, bytes_accessed=6 * MIB, transcendentals=0),
        name="spectra_tail",
    )(x4, taps, table)


VOLT_SHAPE = (2, GROUPS, 2, 64, 128)


def spectra_main(x4, taps, table):
    return pl.pallas_call(
        main_kernel,
        grid=(NFFT // NT,),
        in_specs=slab_specs(FRAMES, 0),
        out_specs=[
            pl.BlockSpec((2, GROUPS, 1, 64, 128), lambda i: (0, 0, 1, 0, 0)),
            pl.BlockSpec((HALF, SIG, COLS), lambda i: (0, 0, 0)),
        ],
        out_shape=[
            jax.ShapeDtypeStruct(VOLT_SHAPE, jnp.bfloat16),
            jax.ShapeDtypeStruct((HALF, SIG, COLS), jnp.float32),
        ],
        scratch_shapes=[filt_shape(FRAMES), acc_shape(FRAMES), turn_shape()],
        compiler_params=params(),
        cost_estimate=pl.CostEstimate(flops=2_600_000_000, bytes_accessed=12 * MIB, transcendentals=0),
        name="spectra_main",
    )(x4, taps, table)


def spectra_join(early, halo, late):
    return pl.pallas_call(
        join_kernel,
        grid=(1,),
        in_specs=[
            pl.BlockSpec((HALF, SIG, COLS), lambda i: (0, 0, 0)),
            pl.BlockSpec((HALF, SIG, COLS), lambda i: (0, 0, 0)),
            pl.BlockSpec(memory_space=pl.ANY),
        ],
        out_specs=pl.BlockSpec((2, GROUPS, 1, 64, 128), lambda i: (0, 0, 0, 0, 0)),
        out_shape=jax.ShapeDtypeStruct(VOLT_SHAPE, jnp.bfloat16),
        scratch_shapes=[turn_shape()],
        input_output_aliases={2: 0},
        compiler_params=params(),
        cost_estimate=pl.CostEstimate(flops=1_000_000, bytes_accessed=3 * MIB, transcendentals=0),
        name="spectra_join",
    )(early, halo, late)


def gather(j, own_ref, other_ref, all_ref, q):
    at = slice(q * 2 * SIG, (q + 1) * 2 * SIG)
    for c, ref in enumerate((own_ref, other_ref)):
        for y in range(2):
            for h in range(2):
                t0 = ref[y * GROUPS + 2 * q, h, j]
                t1 = ref[y * GROUPS + 2 * q + 1, h, j]
                even = jnp.concatenate([t0[:, :SIG], t1[:, :SIG]], axis=1)
                odd = jnp.concatenate([t0[:, SIG:], t1[:, SIG:]], axis=1)
                k = ((c * 2 + y) * 2 + h) * 16
                all_ref[k : k + 16, at] = jnp.concatenate([even[:8], odd[:8]], axis=0)
                all_ref[128 + k : 144 + k, at] = jnp.concatenate([even[8:], odd[8:]], axis=0)


def turn(tm_ref, all_ref, left_ref):
    mine = pl.ds(pl.multiple_of(tm_ref[0] * 512, 512), 512)
    rows = all_ref[:, mine].T
    left_ref[:512] = rows
    left_ref[512:, :128] = rows[:, 128:]
    left_ref[512:, 128:] = -rows[:, :128]


def correlate_kernel(scale, tm_ref, own_ref, other_ref, o_ref, *scratch):
    alls, lefts, stages, sem = scratch[:2], scratch[2:4], scratch[4:6], scratch[6]
    tiles = o_ref.shape[-1] // 256
    pairs = GROUPS // 2 // tiles
    flying = {}
    for q in range(GROUPS // 2):
        gather(0, own_ref, other_ref, alls[0], q)
    turn(tm_ref, alls[0], lefts[0])
    for j in range(CH_DEV):
        slot, other_slot = j % 2, (j + 1) % 2
        stage = stages[slot]
        for n in range(tiles):
            cols = slice(n * 256, n * 256 + 256)
            piece = n // SEND
            if n % SEND == 0 and (slot, piece) in flying:
                flying.pop((slot, piece)).wait()
            both = jnp.dot(
                lefts[slot][...], alls[slot][:, cols], preferred_element_type=jnp.float32
            )
            both = (both * scale).astype(jnp.bfloat16)
            stage[0, :, cols] = both[:512]
            stage[1, :, cols] = both[512:]
            if j + 1 < CH_DEV:
                for q in range(n * pairs, (n + 1) * pairs):
                    gather(j + 1, own_ref, other_ref, alls[other_slot], q)
            if n % SEND == SEND - 1:
                wide = slice(piece * SEND * 256, (piece + 1) * SEND * 256)
                copy = pltpu.make_async_copy(
                    stage.at[:, :, wide], o_ref.at[j, :, :, wide], sem.at[slot, piece]
                )
                copy.start()
                flying[slot, piece] = copy
        if j + 1 < CH_DEV:
            turn(tm_ref, alls[other_slot], lefts[other_slot])
    for copy in flying.values():
        copy.wait()


def correlate(tm, own, other, signals, frames_all):
    shape = (2 * GROUPS, 2, CH_DEV, 16, 128)
    return pl.pallas_call(
        functools.partial(correlate_kernel, 1.0 / frames_all),
        in_specs=[
            pl.BlockSpec(memory_space=pltpu.SMEM),
            pl.BlockSpec(memory_space=pltpu.VMEM),
            pl.BlockSpec(memory_space=pltpu.VMEM),
        ],
        out_specs=pl.BlockSpec(memory_space=pl.ANY),
        out_shape=jax.ShapeDtypeStruct((CH_DEV, 2, 512, signals), jnp.bfloat16),
        scratch_shapes=[pltpu.VMEM((256, signals), jnp.bfloat16)] * 2
        + [pltpu.VMEM((1024, 256), jnp.bfloat16)] * 2
        + [pltpu.VMEM((2, 512, signals), jnp.bfloat16)] * 2
        + [pltpu.SemaphoreType.DMA((2, signals // 256 // SEND))],
        compiler_params=params(),
        cost_estimate=pl.CostEstimate(flops=4_300_000_000, bytes_accessed=20 * MIB, transcendentals=0),
        name="correlate",
    )(tm, own.reshape(shape), other.reshape(shape))


def per_device(samples, tap_weights):
    x4 = samples.reshape(SIG // 8, 8, FRAMES, NFFT).transpose(0, 2, 1, 3)
    table = dft_columns()
    tail = spectra_tail(x4, tap_weights, table)
    halo = lax.ppermute(tail, ("yh", "core"), [(0, 1), (1, 2), (2, 3)])
    late, early = spectra_main(x4, tap_weights, table)
    volts = spectra_join(early, halo, late)
    volts = volts.reshape(2 * GROUPS, 128, 128)
    own = lax.all_to_all(volts, PEERS, split_axis=0, concat_axis=0, tiled=True)
    other = lax.ppermute(own, "core", [(0, 1), (1, 0)])
    tm = (lax.axis_index("yh") * 2 + lax.axis_index("core")).astype(jnp.int32).reshape(1)
    return correlate(tm, own, other, GROUPS * SIG, FRAMES * 4)


def solution(mesh):
    fine = Mesh(
        mesh.devices.reshape(2, 2, 2, 4, 4),
        ("yh", "core", "yl", "x", "z"),
    )
    return jax.shard_map(
        per_device,
        mesh=fine,
        in_specs=(P(("yl", "x", "z"), ("yh", "core")), P()),
        out_specs=P(("yl", "x", "z"), None, ("yh", "core"), None),
        check_vma=False,
    )
```

```python
import functools
import math

import jax
import jax.numpy as jnp
import numpy as np
from jax import lax
from jax.experimental import pallas as pl
from jax.experimental.pallas import tpu as pltpu
from jax.sharding import Mesh
from jax.sharding import PartitionSpec as P

NFFT = 2048
TAPS = 16
CH0 = 256
CH_DEV = 4
GROUPS = 32
COLS = GROUPS * CH_DEV * 2
SIG = 64
FRAMES = 32
HALF = 16
NT = 512
LANES = 256
SEND = 4
MIB = 2**20
TAIL_MIB = 24
MAIN_MIB = 24
JOIN_MIB = 24
CORR_MIB = 24
PEERS = ("yh", "yl", "x", "z")


def dft_columns():
    col = np.arange(COLS)
    channel = CH0 + col // 2
    m = (np.arange(NFFT)[:, None] * channel[None, :]) % NFFT
    angle = m * (2.0 * math.pi / NFFT)
    table = np.where((col % 2 == 0)[None, :], np.cos(angle), -np.sin(angle)) / math.sqrt(NFFT)
    return jnp.asarray(table.astype(np.float32)).astype(jnp.bfloat16)


def pair_sum(terms):
    terms = list(terms)
    while len(terms) > 1:
        terms = [
            terms[i] + terms[i + 1] if i + 1 < len(terms) else terms[i]
            for i in range(0, len(terms), 2)
        ]
    return terms[0]


def filtered(first_in, count_in, first_out, count_out, x, weights, filt_ref, lanes):
    for s in range(SIG // 8):
        held = {}
        for g in range(first_out, first_out + count_out):
            frames = [f for f in range(g - TAPS + 1, g + 1) if first_in <= f < first_in + count_in]
            held = {f: held[f] if f in held else x(s, f) for f in frames}
            if frames:
                row = pair_sum(held[f] * weights[f - g + TAPS - 1] for f in frames)
            else:
                row = jnp.zeros((8, LANES), jnp.bfloat16)
            filt_ref[g - first_out, s, :, lanes] = row


def accumulate(first_in, count_in, first_out, count_out, i, x_ref, w_ref, filt_ref):
    for n in range(0, NT, LANES):
        at = slice(i * NT + n, i * NT + n + LANES)
        weights = [
            jnp.broadcast_to(w_ref[p : p + 1, at], (8, LANES)).astype(jnp.bfloat16)
            for p in range(TAPS)
        ]
        filtered(
            first_in,
            count_in,
            first_out,
            count_out,
            lambda s, f: x_ref[s, f, :, at],
            weights,
            filt_ref,
            slice(n, n + LANES),
        )


def project(i, count_out, d_ref, filt_ref, acc_ref):
    table = d_ref[i * NT : i * NT + NT, :]
    for k in range(0, count_out, 4):
        part = jnp.dot(
            filt_ref[k : k + 4].reshape(4 * SIG, NT), table, preferred_element_type=jnp.float32
        )
        acc_ref[k : k + 4] += part.reshape(4, SIG, COLS)


def tail_kernel(
    x_ref, w_ref, d_ref, o_ref, x_out, w_out, d_out, filt_ref, acc_ref, sem, early_sem
):
    slabs = NFFT // NT

    def copy(first, i, sems):
        at = slice(i * NT, i * NT + NT)
        return pltpu.make_async_copy(
            x_ref.at[:, first : first + HALF, :, at],
            x_out.at[:, first : first + HALF, :, at],
            sems.at[i],
        )

    w_copy = pltpu.make_async_copy(w_ref, w_out, sem.at[slabs])
    d_copy = pltpu.make_async_copy(d_ref, d_out, sem.at[slabs + 1])
    w_copy.start()
    copy(HALF, 0, sem).start()
    copy(HALF, 1, sem).start()
    d_copy.start()
    acc_ref[...] = jnp.zeros_like(acc_ref)
    w_copy.wait()

    for i in range(slabs):
        copy(HALF, i, sem).wait()
        if i + 2 < slabs:
            copy(HALF, i + 2, sem).start()
        copy(0, i, early_sem).start()
        accumulate(HALF, HALF, FRAMES, HALF, i, x_out, w_out, filt_ref)
        if i == 0:
            d_copy.wait()
        project(i, HALF, d_out, filt_ref, acc_ref)
    o_ref[...] = acc_ref[...].astype(o_ref.dtype)
    for i in range(slabs):
        copy(0, i, early_sem).wait()


def emit(acc, turn_ref):
    for k in range(HALF // 2):
        block = acc(2 * k).reshape(2 * SIG, COLS)
        turn_ref[pl.ds(k, COLS, stride=HALF // 2), :] = block.T
    return turn_ref[...].astype(jnp.bfloat16).reshape(GROUPS, 64, 128)


def main_kernel(x_ref, w_ref, d_ref, o_ref, early_ref, filt_ref, acc_ref, turn_ref):
    @pl.when(pl.program_id(0) == 0)
    def _():
        acc_ref[...] = jnp.zeros_like(acc_ref)

    accumulate(0, FRAMES, 0, FRAMES, 0, x_ref, w_ref, filt_ref)
    project(0, FRAMES, d_ref, filt_ref, acc_ref)

    @pl.when(pl.program_id(0) == pl.num_programs(0) - 1)
    def _():
        early_ref[...] = acc_ref[:HALF]
        late = emit(lambda k: acc_ref[HALF + k : HALF + k + 2], turn_ref)
        o_ref[0, :, 0] = late
        o_ref[1, :, 0] = late


def join_kernel(early_ref, halo_ref, late_ref, o_ref, turn_ref):
    del late_ref

    def both(k):
        return early_ref[k : k + 2] + halo_ref[k : k + 2].astype(jnp.float32)

    early = emit(both, turn_ref)
    o_ref[0, :, 0] = early
    o_ref[1, :, 0] = early


def params(mib):
    return pltpu.CompilerParams(vmem_limit_bytes=mib * MIB)


def filt_shape(frames):
    return pltpu.VMEM((frames, SIG // 8, 8, NT), jnp.bfloat16)


def acc_shape(frames):
    return pltpu.VMEM((frames, SIG, COLS), jnp.float32)


def turn_shape():
    return pltpu.VMEM((COLS * HALF // 2, 128), jnp.float32)


VOLT_SHAPE = (2, GROUPS, 2, 64, 128)
VMEM = pl.BlockSpec(memory_space=pltpu.VMEM)


def spectra_tail(x4, taps, table):
    return pl.pallas_call(
        tail_kernel,
        in_specs=[pl.BlockSpec(memory_space=pltpu.HBM)] * 3,
        out_specs=[VMEM] * 4,
        out_shape=[
            jax.ShapeDtypeStruct((HALF, SIG, COLS), jnp.bfloat16),
            jax.ShapeDtypeStruct(x4.shape, x4.dtype),
            jax.ShapeDtypeStruct(taps.shape, taps.dtype),
            jax.ShapeDtypeStruct(table.shape, table.dtype),
        ],
        scratch_shapes=[
            filt_shape(HALF),
            acc_shape(HALF),
            pltpu.SemaphoreType.DMA((NFFT // NT + 2,)),
            pltpu.SemaphoreType.DMA((NFFT // NT,)),
        ],
        compiler_params=params(TAIL_MIB),
        cost_estimate=pl.CostEstimate(flops=600_000_000, bytes_accessed=9 * MIB, transcendentals=0),
        name="spectra_tail",
    )(x4, taps, table)


def spectra_main(x4, taps, table):
    return pl.pallas_call(
        main_kernel,
        grid=(NFFT // NT,),
        in_specs=[
            pl.BlockSpec((SIG // 8, FRAMES, 8, NT), lambda i: (0, 0, 0, i)),
            pl.BlockSpec((TAPS, NT), lambda i: (0, i)),
            pl.BlockSpec((NT, COLS), lambda i: (i, 0)),
        ],
        out_specs=[
            pl.BlockSpec((2, GROUPS, 1, 64, 128), lambda i: (0, 0, 1, 0, 0)),
            pl.BlockSpec((HALF, SIG, COLS), lambda i: (0, 0, 0)),
        ],
        out_shape=[
            jax.ShapeDtypeStruct(VOLT_SHAPE, jnp.bfloat16),
            jax.ShapeDtypeStruct((HALF, SIG, COLS), jnp.float32),
        ],
        scratch_shapes=[filt_shape(FRAMES), acc_shape(FRAMES), turn_shape()],
        compiler_params=params(MAIN_MIB),
        cost_estimate=pl.CostEstimate(flops=2_600_000_000, bytes_accessed=12 * MIB, transcendentals=0),
        name="spectra_main",
    )(x4, taps, table)


def spectra_join(early, halo, late):
    return pl.pallas_call(
        join_kernel,
        in_specs=[VMEM, VMEM, pl.BlockSpec(memory_space=pl.ANY)],
        out_specs=pl.BlockSpec(VOLT_SHAPE[:2] + (1, 64, 128), lambda i: (0, 0, 0, 0, 0)),
        grid=(1,),
        out_shape=jax.ShapeDtypeStruct(VOLT_SHAPE, jnp.bfloat16),
        scratch_shapes=[turn_shape()],
        input_output_aliases={2: 0},
        compiler_params=params(JOIN_MIB),
        cost_estimate=pl.CostEstimate(flops=1_000_000, bytes_accessed=3 * MIB, transcendentals=0),
        name="spectra_join",
    )(early, halo, late)


def gather(c, t, all_ref, q):
    at = slice(q * 2 * SIG, (q + 1) * 2 * SIG)
    for y in range(2):
        for h in range(2):
            t0 = t(y, 2 * q, h)
            t1 = t(y, 2 * q + 1, h)
            even = jnp.concatenate([t0[:, :SIG], t1[:, :SIG]], axis=1)
            odd = jnp.concatenate([t0[:, SIG:], t1[:, SIG:]], axis=1)
            k = ((c * 2 + y) * 2 + h) * 16
            all_ref[k : k + 16, at] = jnp.concatenate([even[:8], odd[:8]], axis=0)
            all_ref[128 + k : 144 + k, at] = jnp.concatenate([even[8:], odd[8:]], axis=0)


def turn(tm_ref, all_ref, left_ref):
    mine = pl.ds(pl.multiple_of(tm_ref[0] * 512, 512), 512)
    rows = all_ref[:, mine].T
    left_ref[:512] = rows
    left_ref[512:, :128] = rows[:, 128:]
    left_ref[512:, 128:] = -rows[:, :128]


def correlate_kernel(scale, tm_ref, own_ref, other_ref, o_ref, *scratch):
    alls, lefts, stages = scratch[:2], scratch[2:4], scratch[4:6]
    held_ref, sem, held_sem = scratch[6:]
    tiles = o_ref.shape[-1] // 256
    pairs = GROUPS // 2 // tiles
    flying = {}
    copies = [
        pltpu.make_async_copy(other_ref.at[:, :, j], held_ref.at[j], held_sem.at[j])
        for j in range(CH_DEV)
    ]
    for copy in copies:
        copy.start()

    def bring(j, c, q):
        if c == 0:
            gather(c, lambda y, g, h: own_ref[y * GROUPS + g, h, j], alls[j % 2], q)
        else:
            gather(c, lambda y, g, h: held_ref[j, y * GROUPS + g, h], alls[j % 2], q)

    for q in range(GROUPS // 2):
        bring(0, 0, q)
    copies[0].wait()
    for q in range(GROUPS // 2):
        bring(0, 1, q)
    turn(tm_ref, alls[0], lefts[0])
    for j in range(CH_DEV):
        slot, other_slot = j % 2, (j + 1) % 2
        stage = stages[slot]
        if j + 1 < CH_DEV:
            copies[j + 1].wait()
        for n in range(tiles):
            cols = slice(n * 256, n * 256 + 256)
            piece = n // SEND
            if n % SEND == 0 and (slot, piece) in flying:
                flying.pop((slot, piece)).wait()
            both = jnp.dot(
                lefts[slot][...], alls[slot][:, cols], preferred_element_type=jnp.float32
            )
            both = (both * scale).astype(jnp.bfloat16)
            stage[0, :, cols] = both[:512]
            stage[1, :, cols] = both[512:]
            if j + 1 < CH_DEV:
                for q in range(n * pairs, (n + 1) * pairs):
                    bring(j + 1, 0, q)
                    bring(j + 1, 1, q)
            if n % SEND == SEND - 1:
                wide = slice(piece * SEND * 256, (piece + 1) * SEND * 256)
                copy = pltpu.make_async_copy(
                    stage.at[:, :, wide], o_ref.at[j, :, :, wide], sem.at[slot, piece]
                )
                copy.start()
                flying[slot, piece] = copy
        if j + 1 < CH_DEV:
            turn(tm_ref, alls[other_slot], lefts[other_slot])
    for copy in flying.values():
        copy.wait()


def correlate(tm, own, other, signals, frames_all):
    shape = (2 * GROUPS, 2, CH_DEV, 16, 128)
    return pl.pallas_call(
        functools.partial(correlate_kernel, 1.0 / frames_all),
        in_specs=[
            pl.BlockSpec(memory_space=pltpu.SMEM),
            VMEM,
            pl.BlockSpec(memory_space=pl.ANY),
        ],
        out_specs=pl.BlockSpec(memory_space=pl.ANY),
        out_shape=jax.ShapeDtypeStruct((CH_DEV, 2, 512, signals), jnp.bfloat16),
        scratch_shapes=[pltpu.VMEM((256, signals), jnp.bfloat16)] * 2
        + [pltpu.VMEM((1024, 256), jnp.bfloat16)] * 2
        + [pltpu.VMEM((2, 512, signals), jnp.bfloat16)] * 2
        + [
            pltpu.VMEM((CH_DEV, 2 * GROUPS, 2, 16, 128), jnp.bfloat16),
            pltpu.SemaphoreType.DMA((2, signals // 256 // SEND)),
            pltpu.SemaphoreType.DMA((CH_DEV,)),
        ],
        compiler_params=params(CORR_MIB),
        cost_estimate=pl.CostEstimate(flops=4_300_000_000, bytes_accessed=20 * MIB, transcendentals=0),
        name="correlate",
    )(tm, own.reshape(shape), other.reshape(shape))


def front(samples, tap_weights, send):
    x4 = samples.reshape(SIG // 8, 8, FRAMES, NFFT).transpose(0, 2, 1, 3)
    operands = [pltpu.with_memory_space_constraint(v, pltpu.HBM) for v in (x4, tap_weights, dft_columns())]
    tail, *held = spectra_tail(*operands)
    halo = send(tail)
    late, early = spectra_main(*held)
    return spectra_join(early, halo, late).reshape(2 * GROUPS, 128, 128)


def per_device(samples, tap_weights):
    volts = front(
        samples,
        tap_weights,
        lambda v: lax.ppermute(v, ("yh", "core"), [(0, 1), (1, 2), (2, 3)]),
    )
    own = lax.all_to_all(volts, PEERS, split_axis=0, concat_axis=0, tiled=True)
    other = lax.ppermute(own, "core", [(0, 1), (1, 0)])
    tm = (lax.axis_index("yh") * 2 + lax.axis_index("core")).astype(jnp.int32).reshape(1)
    return correlate(tm, own, other, GROUPS * SIG, FRAMES * 4)


def solution(mesh):
    fine = Mesh(
        mesh.devices.reshape(2, 2, 2, 4, 4),
        ("yh", "core", "yl", "x", "z"),
    )
    return jax.shard_map(
        per_device,
        mesh=fine,
        in_specs=(P(("yl", "x", "z"), ("yh", "core")), P()),
        out_specs=P(("yl", "x", "z"), None, ("yh", "core"), None),
        check_vma=False,
    )
```

```python
import functools
import math

import jax
import jax.numpy as jnp
import numpy as np
from jax import lax
from jax.experimental import pallas as pl
from jax.experimental.pallas import tpu as pltpu
from jax.sharding import Mesh
from jax.sharding import PartitionSpec as P

NFFT = 2048
TAPS = 16
CH0 = 256
CH_DEV = 4
GROUPS = 32
COLS = GROUPS * CH_DEV * 2
SIG = 64
FRAMES = 32
HALF = 16
NT = 512
LANES = 256
SEND = 4
MIB = 2**20
TAIL_MIB = 24
MAIN_MIB = 24
JOIN_MIB = 24
CORR_MIB = 24
PEERS = ("yh", "yl", "x", "z")


def dft_columns():
    col = np.arange(COLS)
    channel = CH0 + col // 2
    m = (np.arange(NFFT)[:, None] * channel[None, :]) % NFFT
    angle = m * (2.0 * math.pi / NFFT)
    table = np.where((col % 2 == 0)[None, :], np.cos(angle), -np.sin(angle)) / math.sqrt(NFFT)
    return jnp.asarray(table.astype(np.float32)).astype(jnp.bfloat16)


def pair_sum(terms):
    terms = list(terms)
    while len(terms) > 1:
        terms = [
            terms[i] + terms[i + 1] if i + 1 < len(terms) else terms[i]
            for i in range(0, len(terms), 2)
        ]
    return terms[0]


def filtered(first_in, count_in, first_out, count_out, x, weights, filt_ref, lanes):
    for s in range(SIG // 8):
        held = {}
        for g in range(first_out, first_out + count_out):
            frames = [f for f in range(g - TAPS + 1, g + 1) if first_in <= f < first_in + count_in]
            held = {f: held[f] if f in held else x(s, f) for f in frames}
            if frames:
                row = pair_sum(held[f] * weights[f - g + TAPS - 1] for f in frames)
            else:
                row = jnp.zeros((8, LANES), jnp.bfloat16)
            filt_ref[g - first_out, s, :, lanes] = row


def accumulate(first_in, count_in, first_out, count_out, i, x_ref, w_ref, filt_ref):
    for n in range(0, NT, LANES):
        lanes = slice(n, n + LANES)
        weights = [
            jnp.broadcast_to(w_ref[i, p : p + 1, lanes], (8, LANES)).astype(jnp.bfloat16)
            for p in range(TAPS)
        ]
        filtered(
            first_in,
            count_in,
            first_out,
            count_out,
            lambda s, f: x_ref[i, s, f, :, lanes],
            weights,
            filt_ref,
            lanes,
        )


def project(i, count_out, d_ref, filt_ref, acc_ref):
    table = d_ref[i]
    step = min(8, count_out)
    for k in range(0, count_out, step):
        part = jnp.dot(
            filt_ref[k : k + step].reshape(step * SIG, NT), table, preferred_element_type=jnp.float32
        )
        acc_ref[k : k + step] += part.reshape(step, SIG, COLS)


def tail_kernel(
    x_ref, w_ref, d_ref, o_ref, x_out, w_out, d_out, filt_ref, acc_ref, sem, early_sem
):
    slabs = NFFT // NT

    def copy(first, i, sems):
        at = slice(i * NT, i * NT + NT)
        return pltpu.make_async_copy(
            x_ref.at[:, first : first + HALF, :, at],
            x_out.at[i, :, first : first + HALF],
            sems.at[i],
        )

    w_copies = [
        pltpu.make_async_copy(
            w_ref.at[:, slice(i * NT, i * NT + NT)], w_out.at[i], sem.at[slabs + 1 + i]
        )
        for i in range(slabs)
    ]
    d_copy = pltpu.make_async_copy(d_ref, d_out, sem.at[slabs])
    for w_copy in w_copies:
        w_copy.start()
    copy(HALF, 0, sem).start()
    copy(HALF, 1, sem).start()
    d_copy.start()
    acc_ref[...] = jnp.zeros_like(acc_ref)
    for w_copy in w_copies:
        w_copy.wait()

    for i in range(slabs):
        copy(HALF, i, sem).wait()
        if i + 2 < slabs:
            copy(HALF, i + 2, sem).start()
        copy(0, i, early_sem).start()
        accumulate(HALF, HALF, FRAMES, HALF, i, x_out, w_out, filt_ref)
        if i == 0:
            d_copy.wait()
        project(i, HALF, d_out, filt_ref, acc_ref)
    o_ref[...] = acc_ref[...].astype(o_ref.dtype)
    for i in range(slabs):
        copy(0, i, early_sem).wait()


def emit(acc, turn_ref):
    for k in range(HALF // 2):
        block = acc(2 * k).reshape(2 * SIG, COLS)
        turn_ref[pl.ds(k, COLS, stride=HALF // 2), :] = block.T
    return turn_ref[...].astype(jnp.bfloat16).reshape(GROUPS, 64, 128)


def main_kernel(x_ref, w_ref, d_ref, o_ref, early_ref, filt_ref, acc_ref, turn_ref):
    acc_ref[...] = jnp.zeros_like(acc_ref)

    def slab(i, carry):
        accumulate(0, FRAMES, 0, FRAMES, i, x_ref, w_ref, filt_ref)
        project(i, FRAMES, d_ref, filt_ref, acc_ref)
        return carry

    lax.fori_loop(0, NFFT // NT, slab, 0, unroll=2)
    early_ref[...] = acc_ref[:HALF]
    late = emit(lambda k: acc_ref[HALF + k : HALF + k + 2], turn_ref)
    o_ref[0, :, 1] = late
    o_ref[1, :, 1] = late


def join_kernel(early_ref, halo_ref, late_ref, o_ref, turn_ref):
    del late_ref

    def both(k):
        return early_ref[k : k + 2] + halo_ref[k : k + 2].astype(jnp.float32)

    early = emit(both, turn_ref)
    o_ref[0, :, 0] = early
    o_ref[1, :, 0] = early


def params(mib):
    return pltpu.CompilerParams(vmem_limit_bytes=mib * MIB)


def filt_shape(frames):
    return pltpu.VMEM((frames, SIG // 8, 8, NT), jnp.bfloat16)


def acc_shape(frames):
    return pltpu.VMEM((frames, SIG, COLS), jnp.float32)


def turn_shape():
    return pltpu.VMEM((COLS * HALF // 2, 128), jnp.float32)


VOLT_SHAPE = (2, GROUPS, 2, 64, 128)
VMEM = pl.BlockSpec(memory_space=pltpu.VMEM)


def spectra_tail(x4, taps, table):
    return pl.pallas_call(
        tail_kernel,
        in_specs=[pl.BlockSpec(memory_space=pltpu.HBM)] * 3,
        out_specs=[VMEM] * 4,
        out_shape=[
            jax.ShapeDtypeStruct((HALF, SIG, COLS), jnp.bfloat16),
            jax.ShapeDtypeStruct((NFFT // NT,) + x4.shape[:3] + (NT,), x4.dtype),
            jax.ShapeDtypeStruct((NFFT // NT, TAPS, NT), taps.dtype),
            jax.ShapeDtypeStruct(table.shape, table.dtype),
        ],
        scratch_shapes=[
            filt_shape(HALF),
            acc_shape(HALF),
            pltpu.SemaphoreType.DMA((2 * NFFT // NT + 1,)),
            pltpu.SemaphoreType.DMA((NFFT // NT,)),
        ],
        compiler_params=params(TAIL_MIB),
        cost_estimate=pl.CostEstimate(flops=600_000_000, bytes_accessed=9 * MIB, transcendentals=0),
        name="spectra_tail",
    )(x4, taps, table)


def spectra_main(x, taps, table):
    return pl.pallas_call(
        main_kernel,
        in_specs=[VMEM] * 3,
        out_specs=[VMEM] * 2,
        out_shape=[
            jax.ShapeDtypeStruct(VOLT_SHAPE, jnp.bfloat16),
            jax.ShapeDtypeStruct((HALF, SIG, COLS), jnp.float32),
        ],
        scratch_shapes=[filt_shape(FRAMES), acc_shape(FRAMES), turn_shape()],
        compiler_params=params(MAIN_MIB),
        cost_estimate=pl.CostEstimate(flops=2_600_000_000, bytes_accessed=12 * MIB, transcendentals=0),
        name="spectra_main",
    )(x, taps, table)


def spectra_join(early, halo, late):
    return pl.pallas_call(
        join_kernel,
        in_specs=[VMEM, VMEM, pl.BlockSpec(memory_space=pl.ANY)],
        out_specs=pl.BlockSpec(VOLT_SHAPE[:2] + (1, 64, 128), lambda i: (0, 0, 0, 0, 0)),
        grid=(1,),
        out_shape=jax.ShapeDtypeStruct(VOLT_SHAPE, jnp.bfloat16),
        scratch_shapes=[turn_shape()],
        input_output_aliases={2: 0},
        compiler_params=params(JOIN_MIB),
        cost_estimate=pl.CostEstimate(flops=1_000_000, bytes_accessed=3 * MIB, transcendentals=0),
        name="spectra_join",
    )(early, halo, late)


def gather(c, t, all_ref, q):
    at = slice(q * 2 * SIG, (q + 1) * 2 * SIG)
    for y in range(2):
        for h in range(2):
            t0 = t(y, 2 * q, h)
            t1 = t(y, 2 * q + 1, h)
            even = jnp.concatenate([t0[:, :SIG], t1[:, :SIG]], axis=1)
            odd = jnp.concatenate([t0[:, SIG:], t1[:, SIG:]], axis=1)
            k = ((c * 2 + y) * 2 + h) * 16
            all_ref[k : k + 16, at] = jnp.concatenate([even[:8], odd[:8]], axis=0)
            all_ref[128 + k : 144 + k, at] = jnp.concatenate([even[8:], odd[8:]], axis=0)


def turn(tm_ref, all_ref, left_ref):
    mine = pl.ds(pl.multiple_of(tm_ref[0] * 512, 512), 512)
    rows = all_ref[:, mine].T
    left_ref[:512] = rows
    left_ref[512:, :128] = rows[:, 128:]
    left_ref[512:, 128:] = -rows[:, :128]


def correlate_kernel(scale, tm_ref, own_ref, other_ref, o_ref, *scratch):
    alls, lefts, stages = scratch[:2], scratch[2:4], scratch[4:6]
    held_ref, sem, held_sem = scratch[6:]
    tiles = o_ref.shape[-1] // 256
    pairs = GROUPS // 2 // tiles
    flying = {}
    copies = [
        pltpu.make_async_copy(other_ref.at[:, :, j], held_ref.at[j], held_sem.at[j])
        for j in range(CH_DEV)
    ]
    for copy in copies:
        copy.start()

    def bring(j, c, q):
        if c == 0:
            gather(c, lambda y, g, h: own_ref[y * GROUPS + g, h, j], alls[j % 2], q)
        else:
            gather(c, lambda y, g, h: held_ref[j, y * GROUPS + g, h], alls[j % 2], q)

    for q in range(GROUPS // 2):
        bring(0, 0, q)
    copies[0].wait()
    for q in range(GROUPS // 2):
        bring(0, 1, q)
    turn(tm_ref, alls[0], lefts[0])
    for j in range(CH_DEV):
        slot, other_slot = j % 2, (j + 1) % 2
        stage = stages[slot]
        if j + 1 < CH_DEV:
            copies[j + 1].wait()
        for n in range(tiles):
            cols = slice(n * 256, n * 256 + 256)
            piece = n // SEND
            if n % SEND == 0 and (slot, piece) in flying:
                flying.pop((slot, piece)).wait()
            both = jnp.dot(
                lefts[slot][...], alls[slot][:, cols], preferred_element_type=jnp.float32
            )
            both = (both * scale).astype(jnp.bfloat16)
            stage[0, :, cols] = both[:512]
            stage[1, :, cols] = both[512:]
            if j + 1 < CH_DEV:
                for q in range(n * pairs, (n + 1) * pairs):
                    bring(j + 1, 0, q)
                    bring(j + 1, 1, q)
            if n % SEND == SEND - 1:
                wide = slice(piece * SEND * 256, (piece + 1) * SEND * 256)
                copy = pltpu.make_async_copy(
                    stage.at[:, :, wide], o_ref.at[j, :, :, wide], sem.at[slot, piece]
                )
                copy.start()
                flying[slot, piece] = copy
        if j + 1 < CH_DEV:
            turn(tm_ref, alls[other_slot], lefts[other_slot])
    for copy in flying.values():
        copy.wait()


def correlate(tm, own, other, signals, frames_all):
    shape = (2 * GROUPS, 2, CH_DEV, 16, 128)
    return pl.pallas_call(
        functools.partial(correlate_kernel, 1.0 / frames_all),
        in_specs=[
            pl.BlockSpec(memory_space=pltpu.SMEM),
            VMEM,
            pl.BlockSpec(memory_space=pl.ANY),
        ],
        out_specs=pl.BlockSpec(memory_space=pl.ANY),
        out_shape=jax.ShapeDtypeStruct((CH_DEV, 2, 512, signals), jnp.bfloat16),
        scratch_shapes=[pltpu.VMEM((256, signals), jnp.bfloat16)] * 2
        + [pltpu.VMEM((1024, 256), jnp.bfloat16)] * 2
        + [pltpu.VMEM((2, 512, signals), jnp.bfloat16)] * 2
        + [
            pltpu.VMEM((CH_DEV, 2 * GROUPS, 2, 16, 128), jnp.bfloat16),
            pltpu.SemaphoreType.DMA((2, signals // 256 // SEND)),
            pltpu.SemaphoreType.DMA((CH_DEV,)),
        ],
        compiler_params=params(CORR_MIB),
        cost_estimate=pl.CostEstimate(flops=4_300_000_000, bytes_accessed=20 * MIB, transcendentals=0),
        name="correlate",
    )(tm, own.reshape(shape), other.reshape(shape))


def front(samples, tap_weights, send):
    x4 = samples.reshape(SIG // 8, 8, FRAMES, NFFT).transpose(0, 2, 1, 3)
    table = dft_columns().reshape(NFFT // NT, NT, COLS)
    operands = [
        pltpu.with_memory_space_constraint(v, pltpu.HBM) for v in (x4, tap_weights, table)
    ]
    tail, *held = spectra_tail(*operands)
    halo = send(tail)
    late, early = spectra_main(*held)
    return spectra_join(early, halo, late).reshape(2 * GROUPS, 128, 128)


def per_device(samples, tap_weights):
    volts = front(
        samples,
        tap_weights,
        lambda v: lax.ppermute(v, ("yh", "core"), [(0, 1), (1, 2), (2, 3)]),
    )
    own = lax.all_to_all(volts, PEERS, split_axis=0, concat_axis=0, tiled=True)
    other = lax.ppermute(own, "core", [(0, 1), (1, 0)])
    tm = (lax.axis_index("yh") * 2 + lax.axis_index("core")).astype(jnp.int32).reshape(1)
    return correlate(tm, own, other, GROUPS * SIG, FRAMES * 4)


def solution(mesh):
    fine = Mesh(
        mesh.devices.reshape(2, 2, 2, 4, 4),
        ("yh", "core", "yl", "x", "z"),
    )
    return jax.shard_map(
        per_device,
        mesh=fine,
        in_specs=(P(("yl", "x", "z"), ("yh", "core")), P()),
        out_specs=P(("yl", "x", "z"), None, ("yh", "core"), None),
        check_vma=False,
    )
```

```python
import functools
import math

import jax
import jax.numpy as jnp
import numpy as np
from jax import lax
from jax.experimental import pallas as pl
from jax.experimental.pallas import tpu as pltpu
from jax.sharding import Mesh
from jax.sharding import PartitionSpec as P

NFFT = 2048
TAPS = 16
CH0 = 256
CH_DEV = 4
GROUPS = 32
COLS = GROUPS * CH_DEV * 2
SIG = 64
FRAMES = 32
HALF = 16
NT = 512
LANES = 256
SEND = 4
MIB = 2**20
TAIL_MIB = 24
MAIN_MIB = 24
JOIN_MIB = 24
CORR_MIB = 24
PEERS = ("yh", "yl", "x", "z")


def dft_columns():
    col = np.arange(COLS)
    channel = CH0 + col // 2
    m = (np.arange(NFFT)[:, None] * channel[None, :]) % NFFT
    angle = m * (2.0 * math.pi / NFFT)
    table = np.where((col % 2 == 0)[None, :], np.cos(angle), -np.sin(angle)) / math.sqrt(NFFT)
    return jnp.asarray(table.astype(np.float32)).astype(jnp.bfloat16)


def pair_sum(terms):
    terms = list(terms)
    while len(terms) > 1:
        terms = [
            terms[i] + terms[i + 1] if i + 1 < len(terms) else terms[i]
            for i in range(0, len(terms), 2)
        ]
    return terms[0]


def filtered(first_in, count_in, first_out, count_out, x, weights, filt_ref, lanes):
    for s in range(SIG // 8):
        held = {}
        for g in range(first_out, first_out + count_out):
            frames = [f for f in range(g - TAPS + 1, g + 1) if first_in <= f < first_in + count_in]
            held = {f: held[f] if f in held else x(s, f) for f in frames}
            if frames:
                row = pair_sum(held[f] * weights[f - g + TAPS - 1] for f in frames)
            else:
                row = jnp.zeros((8, LANES), jnp.bfloat16)
            filt_ref[g - first_out, s, :, lanes] = row


def accumulate(first_in, count_in, first_out, count_out, i, x_ref, w_ref, filt_ref):
    for n in range(0, NT, LANES):
        lanes = slice(n, n + LANES)
        weights = [
            jnp.broadcast_to(w_ref[i, p : p + 1, lanes], (8, LANES)).astype(jnp.bfloat16)
            for p in range(TAPS)
        ]
        filtered(
            first_in,
            count_in,
            first_out,
            count_out,
            lambda s, f: x_ref[i, s, f, :, lanes],
            weights,
            filt_ref,
            lanes,
        )


def project(i, count_out, d_ref, filt_ref, acc_ref):
    table = d_ref[i]
    step = min(8, count_out)
    for k in range(0, count_out, step):
        part = jnp.dot(
            filt_ref[k : k + step].reshape(step * SIG, NT), table, preferred_element_type=jnp.float32
        )
        acc_ref[k : k + step] += part.reshape(step, SIG, COLS)


def tail_kernel(
    x_ref, w_ref, d_ref, o_ref, x_out, w_out, d_out, filt_ref, acc_ref, sem, early_sem
):
    slabs = NFFT // NT

    def copy(first, i, sems):
        at = slice(i * NT, i * NT + NT)
        return pltpu.make_async_copy(
            x_ref.at[:, first : first + HALF, :, at],
            x_out.at[i, :, first : first + HALF],
            sems.at[i],
        )

    w_copies = [
        pltpu.make_async_copy(
            w_ref.at[:, slice(i * NT, i * NT + NT)], w_out.at[i], sem.at[slabs + 1 + i]
        )
        for i in range(slabs)
    ]
    d_copy = pltpu.make_async_copy(d_ref, d_out, sem.at[slabs])
    for w_copy in w_copies:
        w_copy.start()
    copy(HALF, 0, sem).start()
    copy(HALF, 1, sem).start()
    d_copy.start()
    acc_ref[...] = jnp.zeros_like(acc_ref)
    for w_copy in w_copies:
        w_copy.wait()

    for i in range(slabs):
        copy(HALF, i, sem).wait()
        if i + 2 < slabs:
            copy(HALF, i + 2, sem).start()
        copy(0, i, early_sem).start()
        accumulate(HALF, HALF, FRAMES, HALF, i, x_out, w_out, filt_ref)
        if i == 0:
            d_copy.wait()
        project(i, HALF, d_out, filt_ref, acc_ref)
    o_ref[...] = acc_ref[: HALF - 1].astype(o_ref.dtype)
    for i in range(slabs):
        copy(0, i, early_sem).wait()


def emit(acc, turn_ref):
    for k in range(HALF // 2):
        block = acc(2 * k).reshape(2 * SIG, COLS)
        turn_ref[pl.ds(k, COLS, stride=HALF // 2), :] = block.T
    return turn_ref[...].astype(jnp.bfloat16).reshape(GROUPS, 64, 128)


def main_kernel(x_ref, w_ref, d_ref, o_ref, early_ref, filt_ref, acc_ref, turn_ref):
    acc_ref[...] = jnp.zeros_like(acc_ref)

    def slab(i, carry):
        accumulate(0, FRAMES, 0, FRAMES, i, x_ref, w_ref, filt_ref)
        project(i, FRAMES, d_ref, filt_ref, acc_ref)
        return carry

    lax.fori_loop(0, NFFT // NT, slab, 0, unroll=2)
    early_ref[...] = acc_ref[:HALF]
    late = emit(lambda k: acc_ref[HALF + k : HALF + k + 2], turn_ref)
    o_ref[0, :, 1] = late
    o_ref[1, :, 1] = late


def join_kernel(early_ref, halo_ref, late_ref, o_ref, turn_ref):
    del late_ref

    def both(k):
        if k + 2 == HALF:
            last = early_ref[k : k + 1] + halo_ref[k : k + 1].astype(jnp.float32)
            return jnp.concatenate([last, early_ref[k + 1 : k + 2]], axis=0)
        return early_ref[k : k + 2] + halo_ref[k : k + 2].astype(jnp.float32)

    early = emit(both, turn_ref)
    o_ref[0, :, 0] = early
    o_ref[1, :, 0] = early


def params(mib):
    return pltpu.CompilerParams(vmem_limit_bytes=mib * MIB)


def filt_shape(frames):
    return pltpu.VMEM((frames, SIG // 8, 8, NT), jnp.bfloat16)


def acc_shape(frames):
    return pltpu.VMEM((frames, SIG, COLS), jnp.float32)


def turn_shape():
    return pltpu.VMEM((COLS * HALF // 2, 128), jnp.float32)


VOLT_SHAPE = (2, GROUPS, 2, 64, 128)
VMEM = pl.BlockSpec(memory_space=pltpu.VMEM)


def spectra_tail(x4, taps, table):
    return pl.pallas_call(
        tail_kernel,
        in_specs=[pl.BlockSpec(memory_space=pltpu.HBM)] * 3,
        out_specs=[VMEM] * 4,
        out_shape=[
            jax.ShapeDtypeStruct((HALF - 1, SIG, COLS), jnp.bfloat16),
            jax.ShapeDtypeStruct((NFFT // NT,) + x4.shape[:3] + (NT,), x4.dtype),
            jax.ShapeDtypeStruct((NFFT // NT, TAPS, NT), taps.dtype),
            jax.ShapeDtypeStruct(table.shape, table.dtype),
        ],
        scratch_shapes=[
            filt_shape(HALF),
            acc_shape(HALF),
            pltpu.SemaphoreType.DMA((2 * NFFT // NT + 1,)),
            pltpu.SemaphoreType.DMA((NFFT // NT,)),
        ],
        compiler_params=params(TAIL_MIB),
        cost_estimate=pl.CostEstimate(flops=600_000_000, bytes_accessed=9 * MIB, transcendentals=0),
        name="spectra_tail",
    )(x4, taps, table)


def spectra_main(x, taps, table):
    return pl.pallas_call(
        main_kernel,
        in_specs=[VMEM] * 3,
        out_specs=[VMEM] * 2,
        out_shape=[
            jax.ShapeDtypeStruct(VOLT_SHAPE, jnp.bfloat16),
            jax.ShapeDtypeStruct((HALF, SIG, COLS), jnp.float32),
        ],
        scratch_shapes=[filt_shape(FRAMES), acc_shape(FRAMES), turn_shape()],
        compiler_params=params(MAIN_MIB),
        cost_estimate=pl.CostEstimate(flops=2_600_000_000, bytes_accessed=12 * MIB, transcendentals=0),
        name="spectra_main",
    )(x, taps, table)


def spectra_join(early, halo, late):
    return pl.pallas_call(
        join_kernel,
        in_specs=[VMEM, VMEM, pl.BlockSpec(memory_space=pl.ANY)],
        out_specs=pl.BlockSpec(VOLT_SHAPE[:2] + (1, 64, 128), lambda i: (0, 0, 0, 0, 0)),
        grid=(1,),
        out_shape=jax.ShapeDtypeStruct(VOLT_SHAPE, jnp.bfloat16),
        scratch_shapes=[turn_shape()],
        input_output_aliases={2: 0},
        compiler_params=params(JOIN_MIB),
        cost_estimate=pl.CostEstimate(flops=1_000_000, bytes_accessed=3 * MIB, transcendentals=0),
        name="spectra_join",
    )(early, halo, late)


def gather(c, t, all_ref, q):
    at = slice(q * 2 * SIG, (q + 1) * 2 * SIG)
    for y in range(2):
        for h in range(2):
            t0 = t(y, 2 * q, h)
            t1 = t(y, 2 * q + 1, h)
            even = jnp.concatenate([t0[:, :SIG], t1[:, :SIG]], axis=1)
            odd = jnp.concatenate([t0[:, SIG:], t1[:, SIG:]], axis=1)
            k = ((c * 2 + y) * 2 + h) * 16
            all_ref[k : k + 16, at] = jnp.concatenate([even[:8], odd[:8]], axis=0)
            all_ref[128 + k : 144 + k, at] = jnp.concatenate([even[8:], odd[8:]], axis=0)


def turn(tm_ref, all_ref, left_ref):
    mine = pl.ds(pl.multiple_of(tm_ref[0] * 512, 512), 512)
    rows = all_ref[:, mine].T
    left_ref[:512] = rows
    left_ref[512:, :128] = rows[:, 128:]
    left_ref[512:, 128:] = -rows[:, :128]


def correlate_kernel(scale, tm_ref, own_ref, other_ref, o_ref, *scratch):
    alls, lefts, stages = scratch[:2], scratch[2:4], scratch[4:6]
    held_ref, sem, held_sem = scratch[6:]
    tiles = o_ref.shape[-1] // 256
    pairs = GROUPS // 2 // tiles
    flying = {}
    copies = [
        pltpu.make_async_copy(other_ref.at[:, :, j], held_ref.at[j], held_sem.at[j])
        for j in range(CH_DEV)
    ]
    for copy in copies:
        copy.start()

    def bring(j, c, q):
        if c == 0:
            gather(c, lambda y, g, h: own_ref[y * GROUPS + g, h, j], alls[j % 2], q)
        else:
            gather(c, lambda y, g, h: held_ref[j, y * GROUPS + g, h], alls[j % 2], q)

    for q in range(GROUPS // 2):
        bring(0, 0, q)
    copies[0].wait()
    for q in range(GROUPS // 2):
        bring(0, 1, q)
    turn(tm_ref, alls[0], lefts[0])
    for j in range(CH_DEV):
        slot, other_slot = j % 2, (j + 1) % 2
        stage = stages[slot]
        if j + 1 < CH_DEV:
            copies[j + 1].wait()
        for n in range(tiles):
            cols = slice(n * 256, n * 256 + 256)
            piece = n // SEND
            if n % SEND == 0 and (slot, piece) in flying:
                flying.pop((slot, piece)).wait()
            both = jnp.dot(
                lefts[slot][...], alls[slot][:, cols], preferred_element_type=jnp.float32
            )
            both = (both * scale).astype(jnp.bfloat16)
            stage[0, :, cols] = both[:512]
            stage[1, :, cols] = both[512:]
            if j + 1 < CH_DEV:
                for q in range(n * pairs, (n + 1) * pairs):
                    bring(j + 1, 0, q)
                    bring(j + 1, 1, q)
            if n % SEND == SEND - 1:
                wide = slice(piece * SEND * 256, (piece + 1) * SEND * 256)
                copy = pltpu.make_async_copy(
                    stage.at[:, :, wide], o_ref.at[j, :, :, wide], sem.at[slot, piece]
                )
                copy.start()
                flying[slot, piece] = copy
        if j + 1 < CH_DEV:
            turn(tm_ref, alls[other_slot], lefts[other_slot])
    for copy in flying.values():
        copy.wait()


def correlate(tm, own, other, signals, frames_all):
    shape = (2 * GROUPS, 2, CH_DEV, 16, 128)
    return pl.pallas_call(
        functools.partial(correlate_kernel, 1.0 / frames_all),
        in_specs=[
            pl.BlockSpec(memory_space=pltpu.SMEM),
            VMEM,
            pl.BlockSpec(memory_space=pl.ANY),
        ],
        out_specs=pl.BlockSpec(memory_space=pl.ANY),
        out_shape=jax.ShapeDtypeStruct((CH_DEV, 2, 512, signals), jnp.bfloat16),
        scratch_shapes=[pltpu.VMEM((256, signals), jnp.bfloat16)] * 2
        + [pltpu.VMEM((1024, 256), jnp.bfloat16)] * 2
        + [pltpu.VMEM((2, 512, signals), jnp.bfloat16)] * 2
        + [
            pltpu.VMEM((CH_DEV, 2 * GROUPS, 2, 16, 128), jnp.bfloat16),
            pltpu.SemaphoreType.DMA((2, signals // 256 // SEND)),
            pltpu.SemaphoreType.DMA((CH_DEV,)),
        ],
        compiler_params=params(CORR_MIB),
        cost_estimate=pl.CostEstimate(flops=4_300_000_000, bytes_accessed=20 * MIB, transcendentals=0),
        name="correlate",
    )(tm, own.reshape(shape), other.reshape(shape))


def front(samples, tap_weights, send):
    x4 = samples.reshape(SIG // 8, 8, FRAMES, NFFT).transpose(0, 2, 1, 3)
    table = dft_columns().reshape(NFFT // NT, NT, COLS)
    operands = [
        pltpu.with_memory_space_constraint(v, pltpu.HBM) for v in (x4, tap_weights, table)
    ]
    tail, *held = spectra_tail(*operands)
    halo = send(tail)
    late, early = spectra_main(*held)
    return spectra_join(early, halo, late).reshape(2 * GROUPS, 128, 128)


def per_device(samples, tap_weights):
    volts = front(
        samples,
        tap_weights,
        lambda v: lax.ppermute(v, ("yh", "core"), [(0, 1), (1, 2), (2, 3)]),
    )
    own = lax.all_to_all(volts, PEERS, split_axis=0, concat_axis=0, tiled=True)
    other = lax.ppermute(own, "core", [(0, 1), (1, 0)])
    tm = (lax.axis_index("yh") * 2 + lax.axis_index("core")).astype(jnp.int32).reshape(1)
    return correlate(tm, own, other, GROUPS * SIG, FRAMES * 4)


def solution(mesh):
    fine = Mesh(
        mesh.devices.reshape(2, 2, 2, 4, 4),
        ("yh", "core", "yl", "x", "z"),
    )
    return jax.shard_map(
        per_device,
        mesh=fine,
        in_specs=(P(("yl", "x", "z"), ("yh", "core")), P()),
        out_specs=P(("yl", "x", "z"), None, ("yh", "core"), None),
        check_vma=False,
    )
```
